256 devices in a mesh: seq: 32 (over x_hi, z, core), head: 8 (over x_lo, y).
Axes of the slice: x: 4 (x_hi: 2, x_lo: 2; x = x_hi * 2 + x_lo), y: 4, z: 8, core: 2. Of those that a mesh axis runs over, the one named last changes fastest.
Arguments:
- text_q: bfloat16 [8192, 8192], P(('seq', 'head')), may hold values from -10 to 10
- text_k: bfloat16 [8192, 1024], P(('seq', 'head')), may hold values from -10 to 10
- text_v: bfloat16 [8192, 1024], P(('seq', 'head')), may hold values from -6 to 6
- vision_kv: bfloat16 [32, 2, 1280, 1024], P('seq', None, None, 'head'), may hold values from -10 to 10
- image_here: int32 [32], P('seq'), may hold values from 0 to 1, as said below
- gate: float32 [64], P('head'), may hold values from -2 to 2
Outputs:
- attended: bfloat16 [8192, 8192], P(('seq', 'head'))
The draws below stay inside these ranges and needn't reach their ends.
Inputs may be any that keep to these rules, and one draw needn't show every extreme that they name: After a slot with image_here 1, one of the next 4 slots has image_here 1 unless the sequence ends first; the first 4 slots hold a 1; somewhere exactly 3 slots of 0 lie between two slots of 1.
All inputs are finite; a program needn't handle non-finite values.
Results may differ from the reference program's by a relative error of at most 0.0065.
Values may be sent and summed in bfloat16 or wider, within the bound.
No kernel may reach another device: no remote copies, remote signals or barrier semaphores. Data moves between devices by JAX's collectives and lax.ppermute only.
A program may use at most 128 MiB of HBM per device.

```python
import math
import jax
import jax.numpy as jnp
from jax import lax

HEADS = 64
KV_HEADS = 8
HD = 128
VIS = 1280
RUN = 4
TOKENS = 8192
IMAGES = 32
N_SEQ = 32


def draw_text_q(key, part):
    key = jax.random.fold_in(key, 1)
    values = jnp.clip(1.7 * jax.random.normal(key, (TOKENS, HEADS * HD)), -10.0, 10.0)
    return values.astype(jnp.bfloat16)


def draw_text_k(key, part):
    key = jax.random.fold_in(key, 2)
    values = jnp.clip(1.7 * jax.random.normal(key, (TOKENS, KV_HEADS * HD)), -10.0, 10.0)
    return values.astype(jnp.bfloat16)


def draw_vision_kv(key, part):
    key = jax.random.fold_in(key, 3)
    law_key = jax.random.fold_in(key, 0)
    shape = (IMAGES, 2, VIS, KV_HEADS * HD)
    factors = jnp.array([1.7, 1.0], jnp.float32)[None, :, None, None]
    values = jnp.clip(factors * jax.random.normal(law_key, shape), -10.0, 10.0)
    return values.astype(jnp.bfloat16)


def draw_image_here(key, part):
    key = jax.random.fold_in(key, 5)
    base_law = (jax.random.randint(key, (IMAGES,), 0, 5) < 2).astype(jnp.int32)
    indices = jnp.arange(IMAGES, dtype=jnp.int32)
    middle = IMAGES // 2 - 1
    base_law = jnp.where(indices == 0, 1, base_law)
    base_law = jnp.where((indices > 0) & (indices < RUN), 0, base_law)
    base_law = jnp.where(indices == RUN, 1, base_law)
    base_law = jnp.where(indices == middle, 1, base_law)
    base_law = jnp.where(indices == middle + 1, 0, base_law)

    def advance(gap_count, block_flag):
        forced = (gap_count + 1 >= RUN).astype(jnp.int32)
        has_image = jnp.maximum(block_flag, forced)
        return (jnp.where(has_image > 0, jnp.int32(0), gap_count + 1), has_image)
    _, flags = lax.scan(advance, jnp.int32(RUN), base_law)
    return flags.astype(jnp.int32)


def block_scale(rng, extent, cuts, least, largest):
    def one(position, shards_of):
        steps = jax.random.uniform(jax.random.fold_in(jax.random.fold_in(rng, 6), position), (shards_of,), jnp.float32, least / len(cuts), largest / len(cuts))
        return jnp.repeat(jnp.exp(steps), extent[position] // shards_of).reshape((-1,) + (1,) * (len(extent) - position - 1))

    level = one(*cuts[0])
    for cut in cuts[1:]:
        level = level * one(*cut)
    return level


def gaussian(own_key, shape, width, bound, cuts=(), kind=jnp.bfloat16):
    factor_of = block_scale(own_key, shape, cuts, -0.22, 0.18) if cuts else 1.0
    entries = jax.random.normal(own_key, shape, jnp.float32) * width * factor_of
    return jnp.minimum(jnp.maximum(entries, -bound), bound).astype(kind)


def setup_inputs(seed: int = 0) -> dict:
    keys = jax.random.split(jax.random.key(seed), 7)
    text_q = draw_text_q(jax.random.fold_in(keys[6], 71), 0)
    text_k = draw_text_k(jax.random.fold_in(keys[6], 71), 0)
    text_v = gaussian(keys[2], (TOKENS, KV_HEADS * HD), 1.0, 6.0, ((0, 256),))
    vision_kv = draw_vision_kv(jax.random.fold_in(keys[6], 71), 0)
    image_here = draw_image_here(jax.random.fold_in(keys[6], 71), 0)
    gate = jnp.clip(jax.random.uniform(keys[5], (HEADS,), jnp.float32, -2.0, 2.0) * block_scale(keys[5], (HEADS,), ((0, 8),), -0.4, 0.0), -2.0, 2.0)
    return dict(text_q=text_q, text_k=text_k, text_v=text_v, vision_kv=vision_kv, image_here=image_here, gate=gate)


very_negative = -1e+30

def self_attention(text_q, text_k, text_v):
    per_group = HEADS // KV_HEADS
    block_rows = min(512, TOKENS)
    block_count = TOKENS // block_rows
    score_scale = 1.0 / math.sqrt(HD)
    queries = text_q.reshape(block_count, block_rows, KV_HEADS, per_group, HD).transpose(0, 2, 1, 3, 4)
    keys_all = text_k.reshape(TOKENS, KV_HEADS, HD).transpose(1, 0, 2)
    values_all = text_v.reshape(TOKENS, KV_HEADS, HD).transpose(1, 0, 2)
    key_positions = jnp.arange(TOKENS, dtype=jnp.int32)

    def per_block(entry):
        block_queries, block_position = entry
        query_positions = block_position * block_rows + jnp.arange(block_rows, dtype=jnp.int32)
        allowed = query_positions[:, None] >= key_positions[None, :]

        def per_head(head_entry):
            head_queries, head_keys, head_values = head_entry
            scores = jnp.einsum('qgd,sd->gqs', head_queries.astype(jnp.float32), head_keys.astype(jnp.float32)) * score_scale
            scores = jnp.where(allowed[None], scores, very_negative)
            row_top = lax.optimization_barrier(jnp.max(scores, axis=-1, keepdims=True))
            weights = jnp.where(allowed[None], jnp.exp(scores - row_top), 0.0)
            denominator = lax.optimization_barrier(jnp.sum(weights, axis=-1))
            rounded = lax.optimization_barrier(weights.astype(jnp.bfloat16)).astype(jnp.float32)
            summed = jnp.einsum('gqs,sd->gqd', rounded, head_values.astype(jnp.float32))
            return summed / denominator[..., None]
        return lax.map(per_head, (block_queries, keys_all, values_all))
    outputs = lax.map(per_block, (queries, jnp.arange(block_count, dtype=jnp.int32)))
    return outputs.transpose(0, 3, 1, 2, 4).reshape(TOKENS, HEADS * HD)

def cross_attention(text_q, vision_kv, image_here):
    per_group = HEADS // KV_HEADS
    block_rows = TOKENS // N_SEQ
    score_scale = 1.0 / math.sqrt(HD)
    slots = jnp.where(image_here > 0, jnp.arange(IMAGES, dtype=jnp.int32), jnp.int32(-1))
    latest = lax.cummax(slots)
    seen = (latest >= 0).astype(jnp.float32)
    chosen = jnp.maximum(latest, 0).astype(jnp.int32)
    queries = text_q.reshape(N_SEQ, block_rows, KV_HEADS, per_group, HD)

    def per_block(entry):
        block_queries, image_index = entry
        image = lax.dynamic_index_in_dim(vision_kv, image_index, 0, keepdims=False)
        image_keys = image[0].reshape(VIS, KV_HEADS, HD).astype(jnp.float32)
        image_values = image[1].reshape(VIS, KV_HEADS, HD).astype(jnp.float32)
        scores = jnp.einsum('qkgd,vkd->kgqv', block_queries.astype(jnp.float32), image_keys) * score_scale
        row_top = lax.optimization_barrier(jnp.max(scores, axis=-1, keepdims=True))
        weights = jnp.exp(scores - row_top)
        denominator = lax.optimization_barrier(jnp.sum(weights, axis=-1))
        rounded = lax.optimization_barrier(weights.astype(jnp.bfloat16)).astype(jnp.float32)
        summed = jnp.einsum('kgqv,vkd->kgqd', rounded, image_values) / denominator[..., None]
        return summed.transpose(2, 0, 1, 3).reshape(block_rows, HEADS * HD)
    outputs = lax.map(per_block, (queries, chosen)).reshape(TOKENS, HEADS * HD)
    return outputs * jnp.repeat(seen, block_rows)[:, None]

def reference(text_q, text_k, text_v, vision_kv, image_here, gate):
    self_out = self_attention(text_q, text_k, text_v)
    cross_out = cross_attention(text_q, vision_kv, image_here)
    gates = jnp.repeat(jnp.tanh(gate), HD)
    return (self_out + gates[None, :] * cross_out).astype(jnp.bfloat16)
```

```python
import functools
import math

import jax
import jax.numpy as jnp
from jax import lax
from jax.experimental import pallas as pl
from jax.experimental.pallas import tpu as pltpu
from jax.sharding import PartitionSpec as P

HD = 128
G = 8
EXP2_SCALE = math.log2(math.e) / math.sqrt(HD)
NEG = -1e30
FLAG_ROWS = 16


def scores_of(q, keys):
    return lax.dot_general(q, keys, (((1,), (1,)), ((), ())), preferred_element_type=jnp.float32)


def sweep(rows, q_ref, parts, bufs, read, write):
    kbuf, vbuf = bufs[:2]
    scores, weights, tops = bufs[2:4], bufs[4:6], bufs[6:8]
    half = rows // 2
    spans = []
    at = 0
    for kv, _, _ in parts:
        n = kv.shape[0]
        kbuf[at : at + n] = kv[:, :HD]
        vbuf[at : at + n, :HD] = kv[:, HD:]
        spans.append(slice(at, at + n))
        at += n
    vbuf[:at, HD:] = jnp.ones((at, HD), jnp.bfloat16)

    def place(h, i):
        start = h * rows + i * half
        return pl.ds(start if isinstance(h, int) else pl.multiple_of(start, half), half)

    def score(h, i):
        lanes = h * HD if isinstance(h, int) else pl.multiple_of(h * HD, HD)
        q = q_ref[i * half : (i + 1) * half, pl.ds(lanes, HD)]
        s = scores_of(q, kbuf[:at])
        if parts[0][2]:
            n = spans[0].stop
            row = lax.broadcasted_iota(jnp.int32, (half, n), 0) + i * half
            col = lax.broadcasted_iota(jnp.int32, (half, n), 1)
            scores[i][:, :n] = jnp.where(row >= col, s[:, :n], NEG)
            scores[i][:, n:at] = s[:, n:]
        else:
            scores[i][:, :at] = s

    def soften(h, i):
        old = read(place(h, i))
        top = None if old is None else old[0]
        for (_, valid, _), span in zip(parts, spans):
            t = jnp.broadcast_to(jnp.max(scores[i][:, span], axis=1, keepdims=True), (half, HD))
            if valid is not None:
                t = jnp.where(valid, t, NEG)
            top = t if top is None else jnp.maximum(top, t)
        tops[i][...] = jnp.broadcast_to(top, (half, HD))
        for (_, valid, _), span in zip(parts, spans):
            base = top[:, :1] * EXP2_SCALE
            if valid is not None:
                base = jnp.where(valid, base, -NEG)
            weights[i][:, span] = jnp.exp2(scores[i][:, span] * EXP2_SCALE - base).astype(jnp.bfloat16)

    def gather(h, i):
        pv = jnp.dot(weights[i][:, :at], vbuf[:at], preferred_element_type=jnp.float32)
        total, acc, top = pv[:, HD:], pv[:, :HD], tops[i][...]
        old = read(place(h, i))
        if old is not None:
            factor = jnp.exp2((old[0] - top) * EXP2_SCALE)
            total, acc = old[1] * factor + total, old[2] * factor + acc
        write(h, i, place(h, i), top, total, acc)

    score(0, 0)
    soften(0, 0)
    score(0, 1)

    def head(h, carry):
        gather(h, 0)
        soften(h, 1)
        score(h + 1, 0)
        gather(h, 1)
        soften(h + 1, 0)
        score(h + 1, 1)
        return carry

    for h in range(G - 1):
        head(h, 0)
    gather(G - 1, 0)
    soften(G - 1, 1)
    gather(G - 1, 1)


def scratch(rows, n_keys):
    half = rows // 2
    return [
        pltpu.VMEM((n_keys, HD), jnp.bfloat16),
        pltpu.VMEM((n_keys, 2 * HD), jnp.bfloat16),
        *[pltpu.VMEM((half, n_keys), jnp.float32)] * 2,
        *[pltpu.VMEM((half, n_keys), jnp.bfloat16)] * 2,
        *[pltpu.VMEM((half, HD), jnp.float32)] * 2,
    ]


def self_kernel(shape, valid_ref, q_ref, *refs):
    n_a, n_b, first, last = shape
    refs, bufs = refs[:-8], refs[-8:]
    a_refs, refs = refs[:n_a], refs[n_a:]
    b_refs, refs = refs[:n_b], refs[n_b:]
    rows = q_ref.shape[0]
    half = rows // 2
    if not first:
        acc_in, ml_in, refs = refs[0], refs[1], refs[2:]
    if last:
        cross_ref, out_ref = refs
    else:
        acc_out, ml_out = refs

    def read(at):
        if first:
            return None
        return ml_in[0, at], ml_in[1, at], acc_in[at]

    def write(h, i, at, top, total, acc):
        if last:
            o = acc / total + cross_ref[at]
            lanes = h * HD if isinstance(h, int) else pl.multiple_of(h * HD, HD)
            out_ref[i * half : (i + 1) * half, pl.ds(lanes, HD)] = o.astype(out_ref.dtype)
            return
        acc_out[at] = acc
        ml_out[0, at] = top
        ml_out[1, at] = total

    a = [(r, valid_ref[i] > 0, False) for i, r in enumerate(a_refs)]
    b = [(r, None, False) for r in b_refs]
    if first:
        a[0] = (a_refs[0], None, True)
    any_a = valid_ref[n_a] > 0
    any_b = valid_ref[n_a + 1] > 0

    @pl.when(any_b)
    def _():
        sweep(rows, q_ref, a + b, bufs, read, write)

    @pl.when(jnp.logical_and(jnp.logical_not(any_b), any_a))
    def _():
        sweep(rows, q_ref, a, bufs, read, write)

    if not first:

        @pl.when(jnp.logical_not(jnp.logical_or(any_a, any_b)))
        def _():
            def head(h, carry):
                for i in range(2):
                    at = pl.ds(pl.multiple_of(h * rows + i * half, half), half)
                    top, total, acc = read(at)
                    write(h, i, at, top, total, acc)
                return carry

            lax.fori_loop(0, G, head, 0)


def self_step(valid, q, a, b, state, cross):
    rows = q.shape[0]
    n_keys = sum(x.shape[0] for x in a + b)
    first, last = state is None, cross is not None
    operands = [valid, q, *a, *b]
    if not first:
        operands += list(state)
    if last:
        operands.append(cross)
        outs = jax.ShapeDtypeStruct(q.shape, jnp.bfloat16)
    else:
        outs = [jax.ShapeDtypeStruct((G * rows, HD), jnp.float32), jax.ShapeDtypeStruct((2, G * rows, HD), jnp.float32)]
    whole = pl.BlockSpec(memory_space=pltpu.VMEM)
    return pl.pallas_call(
        functools.partial(self_kernel, (len(a), len(b), first, last)),
        out_shape=outs,
        in_specs=[pl.BlockSpec(memory_space=pltpu.SMEM)] + [whole] * (len(operands) - 1),
        out_specs=whole if last else [whole, whole],
        scratch_shapes=scratch(rows, n_keys),
        compiler_params=pltpu.CompilerParams(vmem_limit_bytes=VMEM),
        cost_estimate=pl.CostEstimate(
            flops=4 * G * rows * n_keys * HD * 2,
            bytes_accessed=2 * G * rows * HD * 8 + n_keys * HD * 4,
            transcendentals=G * rows * n_keys,
        ),
    )(*operands)


VMEM = 32 << 20


def cross_kernel(gate_ref, q_ref, k_ref, v_ref, out_ref, kv, *bufs):
    rows = q_ref.shape[0]
    kv[:, :HD] = k_ref[...]
    kv[:, HD:] = v_ref[...]

    def write(h, i, at, top, total, acc):
        out_ref[at] = acc / total * gate_ref[h]

    sweep(rows, q_ref, [(kv, None, False)], bufs, lambda at: None, write)


def cross_step(gates, q, k, v):
    rows, n = q.shape[0], k.shape[0]
    whole = pl.BlockSpec(memory_space=pltpu.VMEM)
    return pl.pallas_call(
        cross_kernel,
        out_shape=jax.ShapeDtypeStruct((G * rows, HD), jnp.float32),
        in_specs=[pl.BlockSpec(memory_space=pltpu.SMEM)] + [whole] * 3,
        out_specs=whole,
        scratch_shapes=[pltpu.VMEM((n, 2 * HD), jnp.bfloat16)] + scratch(rows, n),
        compiler_params=pltpu.CompilerParams(vmem_limit_bytes=VMEM),
        cost_estimate=pl.CostEstimate(
            flops=4 * G * rows * n * HD * 2,
            bytes_accessed=G * rows * HD * 8 + n * HD * 4,
            transcendentals=G * rows * n,
        ),
    )(gates, q, k, v)


def paths(n_seq, n_ring):
    def at(half, z, core):
        return (half * n_ring + z % n_ring) * 2 + core

    halves, zs = range(n_seq // (2 * n_ring)), range(n_ring)
    swap = [(i, i ^ 1) for i in range(n_seq)]
    up = [(at(x, z, 0), at(x, z + 1, 0)) for x in halves for z in zs]
    down = [(at(x, z, 1), at(x, z - 1, 1)) for x in halves for z in zs]
    over = [(at(0, z, c), at(1, z, c)) for z in zs for c in range(2)]
    return swap, up, down, over


def local(text_q, text_k, text_v, vision_kv, image_here, gate):
    send = lambda v, pairs: lax.ppermute(v, "seq", pairs)
    seq = lax.axis_index("seq")
    core, z, half = seq % 2, (seq // 2) % 8, seq // 16
    swap, up, down, over = paths(32, 8)
    later = [(i, i + 2) for i in range(30)]
    first_core = core == 0

    image = vision_kv[0]
    here = image_here[0] > 0
    flag = lambda f: jnp.full((FLAG_ROWS, HD), f, jnp.bfloat16)
    mine = jnp.where(first_core, image[0], image[1])
    pair = jnp.where(first_core, image[1], image[0])
    n_vis = mine.shape[0]
    got = send(jnp.concatenate([pair, flag(here)]), swap)
    sibling, sibling_here = got[:n_vis], got[n_vis, 0] > 0
    latest = jnp.where(jnp.where(first_core, sibling_here, ~here), sibling, mine)
    one_back = send(jnp.concatenate([latest, flag(here | sibling_here)]), later)

    rows = text_q.shape[0]
    n_head = lax.axis_size("head")
    wide = lambda t: t.reshape(rows, n_head, -1).transpose(1, 0, 2)
    text = jnp.concatenate([wide(text_q), wide(text_k), wide(text_v)], axis=2)
    text = lax.all_to_all(text, "head", split_axis=0, concat_axis=0, tiled=True)
    text = text.reshape(n_head * rows, -1)
    q, kv = text[:, : G * HD], text[:, G * HD :]

    sib = send(kv, swap)
    below = send(kv, over)
    two_back = send(one_back, later)
    a = jnp.concatenate([kv, sib])
    b = jnp.concatenate([below, send(below, swap)])
    ring = up + down
    as_, bs = [], []
    ra, rb = a, b
    for t in range(1, 4):
        ra = send(ra, ring)
        as_.append((ra, send(ra, swap)))
        rb = send(rb, ring)
        bs.append((rb, send(rb, swap)))
    ra, rb = send(ra, up), send(rb, down)
    far = jnp.where(first_core, ra, rb)
    far_sib = send(far, swap)
    a4 = jnp.where(first_core, far, far_sib)
    b4 = jnp.where(first_core, far_sib, far)

    one_here, two_here = one_back[n_vis, 0] > 0, two_back[n_vis, 0] > 0
    carried = jnp.where(one_here, one_back[:n_vis], two_back[:n_vis])
    here0 = jnp.where(first_core, here, sibling_here)
    here1 = jnp.where(first_core, sibling_here, here)
    image0 = jnp.where(first_core, mine, sibling)
    active0 = jnp.where(here0, image0, carried)
    active1 = jnp.where(here1, jnp.where(first_core, sibling, mine), active0)
    seen = one_here | two_here | here0 | jnp.logical_and(~first_core, here1)
    kept = jnp.where(first_core, active0, active1)
    back = send(jnp.where(first_core, active1, active0), swap)
    vis_k = jnp.where(first_core, kept, back)
    vis_v = jnp.where(first_core, back, kept)
    gates = jnp.tanh(gate) * seen.astype(jnp.float32)

    i32 = lambda *v: jnp.stack([jnp.asarray(x, jnp.int32) for x in v])
    upper = half == 1
    state = self_step(i32(1, ~first_core, 1, upper), q, [kv, sib], [b], None, None)
    cross = cross_step(gates, q, vis_k, vis_v)
    for t in range(1, 4):
        ok_up, ok_down = z >= t, z + t >= 8
        own = jnp.where(first_core, ok_up, ok_down)
        other = jnp.where(first_core, ok_down, ok_up)
        valid = i32(own, other, ok_up | ok_down, upper)
        state = self_step(valid, q, list(as_[t - 1]), list(bs[t - 1]), state, None)
    out = self_step(i32(z >= 4, z >= 4, upper), q, [a4], [b4], state, cross)

    out = out.reshape(n_head, rows, -1)
    out = lax.all_to_all(out, "head", split_axis=0, concat_axis=0, tiled=True)
    return out.transpose(1, 0, 2).reshape(rows, -1)


def solution(mesh):
    placed = (
        P(("seq", "head"), None),
        P(("seq", "head"), None),
        P(("seq", "head"), None),
        P("seq", None, None, "head"),
        P("seq"),
        P("head"),
    )
    return jax.shard_map(
        local, mesh=mesh, in_specs=placed, out_specs=P(("seq", "head"), None), check_vma=False
    )
```

```python
import functools
import math

import jax
import jax.numpy as jnp
from jax import lax
from jax.experimental import pallas as pl
from jax.experimental.pallas import tpu as pltpu
from jax.sharding import PartitionSpec as P

HD = 128
G = 8
EXP2_SCALE = math.log2(math.e) / math.sqrt(HD)
NEG = -1e30
FLAG_ROWS = 16
TOKEN = jax.ShapeDtypeStruct((8, 128), jnp.float32)


def scores_of(q, keys):
    return lax.dot_general(q, keys, (((1,), (1,)), ((), ())), preferred_element_type=jnp.float32)


def sweep(rows, q_ref, parts, bufs, read, write):
    kbuf, vbuf = bufs[:2]
    scores, weights, tops = bufs[2:4], bufs[4:6], bufs[6:8]
    half = rows // 2
    spans = []
    at = 0
    for kv, _, _ in parts:
        n = kv.shape[0]
        kbuf[at : at + n] = kv[:, :HD]
        vbuf[at : at + n, :HD] = kv[:, HD:]
        spans.append(slice(at, at + n))
        at += n
    vbuf[:at, HD:] = jnp.ones((at, HD), jnp.bfloat16)

    def place(h, i):
        start = h * rows + i * half
        return pl.ds(start if isinstance(h, int) else pl.multiple_of(start, half), half)

    def score(h, i):
        lanes = h * HD if isinstance(h, int) else pl.multiple_of(h * HD, HD)
        q = q_ref[i * half : (i + 1) * half, pl.ds(lanes, HD)]
        s = scores_of(q, kbuf[:at])
        if parts[0][2] is None:
            scores[i][:, :at] = s
        else:
            for (_, _, ahead), span in zip(parts, spans):
                n = span.stop - span.start
                row = lax.broadcasted_iota(jnp.int32, (half, n), 0) + i * half
                col = lax.broadcasted_iota(jnp.int32, (half, n), 1)
                scores[i][:, span] = jnp.where(row - col >= ahead, s[:, span], NEG)

    def soften(h, i):
        old = read(place(h, i))
        top = None if old is None else old[0]
        for (_, valid, _), span in zip(parts, spans):
            t = jnp.broadcast_to(jnp.max(scores[i][:, span], axis=1, keepdims=True), (half, HD))
            if valid is not None:
                t = jnp.where(valid, t, NEG)
            top = t if top is None else jnp.maximum(top, t)
        tops[i][...] = jnp.broadcast_to(top, (half, HD))
        for (_, valid, _), span in zip(parts, spans):
            base = top[:, :1] * EXP2_SCALE
            if valid is not None:
                base = jnp.where(valid, base, -NEG)
            weights[i][:, span] = jnp.exp2(scores[i][:, span] * EXP2_SCALE - base).astype(jnp.bfloat16)

    def gather(h, i):
        pv = jnp.dot(weights[i][:, :at], vbuf[:at], preferred_element_type=jnp.float32)
        total, acc, top = pv[:, HD:], pv[:, :HD], tops[i][...]
        old = read(place(h, i))
        if old is not None:
            factor = jnp.exp2((old[0] - top) * EXP2_SCALE)
            total, acc = old[1] * factor + total, old[2] * factor + acc
        write(h, i, place(h, i), top, total, acc)

    score(0, 0)
    soften(0, 0)
    score(0, 1)

    def head(h, carry):
        gather(h, 0)
        soften(h, 1)
        score(h + 1, 0)
        gather(h, 1)
        soften(h + 1, 0)
        score(h + 1, 1)
        return carry

    for h in range(G - 1):
        head(h, 0)
    gather(G - 1, 0)
    soften(G - 1, 1)
    gather(G - 1, 1)


def scratch(rows, n_keys):
    half = rows // 2
    return [
        pltpu.VMEM((n_keys, HD), jnp.bfloat16),
        pltpu.VMEM((n_keys, 2 * HD), jnp.bfloat16),
        *[pltpu.VMEM((half, n_keys), jnp.float32)] * 2,
        *[pltpu.VMEM((half, n_keys), jnp.bfloat16)] * 2,
        *[pltpu.VMEM((half, HD), jnp.float32)] * 2,
    ]


def self_kernel(shape, valid_ref, q_ref, *refs):
    n_in, views, first, base = shape
    refs, bufs = refs[:-8], refs[-8:]
    kv_refs, refs = refs[:n_in], refs[n_in:]
    rows = q_ref.shape[0]
    half = rows // 2
    if not first:
        acc_in, ml_in, refs = refs[0], refs[1], refs[3:]
    acc_out, ml_out, token_ref = refs
    token_ref[...] = jnp.zeros_like(token_ref)

    def read(at):
        if first:
            return None
        return ml_in[0, at], ml_in[1, at], acc_in[at]

    def write(h, i, at, top, total, acc):
        acc_out[at] = acc
        ml_out[0, at] = top
        ml_out[1, at] = total

    def parts(group):
        return [
            (
                kv_refs[i].at[start : start + n],
                None if flag is None or first else valid_ref[base + flag] > 0,
                valid_ref[base + flag] if first else None,
            )
            for i, start, n, flag in views[group]
        ]

    any_a = valid_ref[base] > 0
    any_b = valid_ref[base + 1] > 0

    @pl.when(any_b)
    def _():
        sweep(rows, q_ref, parts(0), bufs, read, write)

    @pl.when(jnp.logical_and(jnp.logical_not(any_b), any_a))
    def _():
        sweep(rows, q_ref, parts(1), bufs, read, write)

    if not first:

        @pl.when(jnp.logical_not(jnp.logical_or(any_a, any_b)))
        def _():
            def head(h, carry):
                for i in range(2):
                    at = pl.ds(pl.multiple_of(h * rows + i * half, half), half)
                    top, total, acc = read(at)
                    write(h, i, at, top, total, acc)
                return carry

            lax.fori_loop(0, G, head, 0)


def self_step(valid, base, q, kvs, views, state, token):
    rows = q.shape[0]
    n_keys = sum(v[2] for v in views[0])
    first = state is None
    operands = [valid, q, *kvs]
    if not first:
        operands += list(state[:2])
    if not first:
        operands.append(token)
    outs = [jax.ShapeDtypeStruct((G * rows, HD), jnp.float32), jax.ShapeDtypeStruct((2, G * rows, HD), jnp.float32), TOKEN]
    whole = pl.BlockSpec(memory_space=pltpu.VMEM)
    return pl.pallas_call(
        functools.partial(self_kernel, (len(kvs), views, first, base)),
        out_shape=outs,
        in_specs=[pl.BlockSpec(memory_space=pltpu.SMEM)] + [whole] * (len(operands) - 1),
        out_specs=[whole] * 3,
        scratch_shapes=scratch(rows, n_keys),
        compiler_params=pltpu.CompilerParams(vmem_limit_bytes=VMEM),
        cost_estimate=pl.CostEstimate(
            flops=4 * G * rows * n_keys * HD * 2,
            bytes_accessed=G * 2 * rows * HD * 8 + n_keys * HD * 4,
            transcendentals=G * rows * n_keys,
        ),
    )(*operands)


VMEM = 20 << 20


def flag_of(ref):
    return jnp.max(ref[-FLAG_ROWS:, :].astype(jnp.float32)) > 0


def choose(index, sources, out_ref):
    n = sources[0].shape[0]
    for i, source in enumerate(sources):

        @pl.when(index == i)
        def _():
            out_ref[:n] = source[:n]


def active_kernel(info_ref, mine_ref, got_ref, one_ref, two_ref, keep_ref, back_ref):
    first_core, here = info_ref[0] == 0, info_ref[1] > 0
    there, one, two = flag_of(got_ref), flag_of(one_ref), flag_of(two_ref)
    n = mine_ref.shape[0]
    here0 = jnp.where(first_core, here, there)
    here1 = jnp.where(first_core, there, here)
    sources = (mine_ref, got_ref, one_ref, two_ref)
    carried = jnp.where(one, 2, 3)
    active0 = jnp.where(here0, jnp.where(first_core, 0, 1), carried)
    active1 = jnp.where(here1, jnp.where(first_core, 1, 0), active0)
    choose(jnp.where(first_core, active0, active1), sources, keep_ref)
    choose(jnp.where(first_core, active1, active0), sources, back_ref)
    earlier = jnp.logical_or(jnp.logical_or(one, two), here0)
    seen = jnp.logical_or(earlier, jnp.logical_and(jnp.logical_not(first_core), here1))
    keep_ref[n:] = jnp.full((FLAG_ROWS, HD), seen.astype(jnp.float32), jnp.float32).astype(jnp.bfloat16)


def active_image(info, mine, got, one, two):
    whole = pl.BlockSpec(memory_space=pltpu.VMEM)
    return pl.pallas_call(
        active_kernel,
        out_shape=[jax.ShapeDtypeStruct(x.shape, x.dtype) for x in (got, mine)],
        in_specs=[pl.BlockSpec(memory_space=pltpu.SMEM)] + [whole] * 4,
        out_specs=[whole] * 2,
        compiler_params=pltpu.CompilerParams(vmem_limit_bytes=2 << 20),
        cost_estimate=pl.CostEstimate(flops=0, bytes_accessed=2 << 20, transcendentals=0),
    )(info, mine, got, one, two)


def cross_kernel(info_ref, gate_ref, q_ref, keep_ref, back_ref, acc_ref, ml_ref, out_ref, kv, *bufs):
    rows = q_ref.shape[0]
    half = rows // 2
    n = back_ref.shape[0]
    first_core = info_ref[0] == 0
    seen = jnp.where(flag_of(keep_ref), 1.0, 0.0)

    @pl.when(first_core)
    def _():
        kv[:, :HD] = keep_ref[:n]
        kv[:, HD:] = back_ref[...]

    @pl.when(jnp.logical_not(first_core))
    def _():
        kv[:, :HD] = back_ref[...]
        kv[:, HD:] = keep_ref[:n]

    def write(h, i, at, top, total, acc):
        o = acc_ref[at] / ml_ref[1, at] + acc / total * (gate_ref[h] * seen)
        lanes = h * HD if isinstance(h, int) else pl.multiple_of(h * HD, HD)
        out_ref[i * half : (i + 1) * half, pl.ds(lanes, HD)] = o.astype(out_ref.dtype)

    sweep(rows, q_ref, [(kv, None, None)], bufs, lambda at: None, write)


def cross_step(info, gates, q, keep, back, state):
    rows, n = q.shape[0], back.shape[0]
    whole = pl.BlockSpec(memory_space=pltpu.VMEM)
    return pl.pallas_call(
        cross_kernel,
        out_shape=jax.ShapeDtypeStruct((rows, G * HD), jnp.bfloat16),
        in_specs=[pl.BlockSpec(memory_space=pltpu.SMEM)] * 2 + [whole] * 5,
        out_specs=whole,
        scratch_shapes=[pltpu.VMEM((n, 2 * HD), jnp.bfloat16)] + scratch(rows, n),
        compiler_params=pltpu.CompilerParams(vmem_limit_bytes=VMEM),
        cost_estimate=pl.CostEstimate(
            flops=4 * G * rows * n * HD * 2,
            bytes_accessed=G * rows * HD * 8 + n * HD * 4,
            transcendentals=G * rows * n,
        ),
    )(info, gates, q, keep, back, *state[:2])


def half_kernel(info_ref, load_ref, out_ref):
    n = out_ref.shape[0]
    for core in range(2):

        @pl.when(info_ref[0] == core)
        def _():
            out_ref[...] = load_ref[core * n : (core + 1) * n]


def core_half(info, load):
    whole = pl.BlockSpec(memory_space=pltpu.VMEM)
    return pl.pallas_call(
        half_kernel,
        out_shape=jax.ShapeDtypeStruct((load.shape[0] // 2, load.shape[1]), load.dtype),
        in_specs=[pl.BlockSpec(memory_space=pltpu.SMEM), whole],
        out_specs=whole,
        compiler_params=pltpu.CompilerParams(vmem_limit_bytes=2 << 20),
        cost_estimate=pl.CostEstimate(flops=0, bytes_accessed=1 << 20, transcendentals=0),
    )(info, load)


def paths(n_seq, n_ring):
    def at(half, z, core):
        return (half * n_ring + z % n_ring) * 2 + core

    halves, zs = range(n_seq // (2 * n_ring)), range(n_ring)
    swap = [(i, i ^ 1) for i in range(n_seq)]
    up = [(at(x, z, 0), at(x, z + 1, 0)) for x in halves for z in zs]
    down = [(at(x, z, 1), at(x, z - 1, 1)) for x in halves for z in zs]
    return swap, up, down


def local(text_q, text_k, text_v, vision_kv, image_here, gate):
    send = lambda v, pairs: lax.ppermute(v, "seq", pairs)
    seq = lax.axis_index("seq")
    core, z, half = seq % 2, (seq // 2) % 8, seq // 16
    swap, up, down = paths(32, 8)
    later = [(i, i + 2) for i in range(30)]
    later_still = [(i, i + 4) for i in range(28)]
    first_core = core == 0
    i32 = lambda *v: jnp.stack([jnp.asarray(x, jnp.int32) for x in v])

    rows = text_q.shape[0]
    n_head = lax.axis_size("head")
    wide = lambda t: t.reshape(rows, n_head, -1).transpose(1, 0, 2)
    spread = lambda t: lax.all_to_all(t, "head", split_axis=0, concat_axis=0, tiled=True).reshape(n_head * rows, -1)
    n = n_head * rows
    upper = half == 1
    ahead = [((x * 8 + z) * 2 + c - seq) * n for x in range(2) for c in range(2)]
    def valid_of(*steps):
        some, flags = False, []
        for t in steps:
            ok_up, ok_down = z >= t, z + t >= 8
            own = jnp.where(first_core, ok_up, ok_down)
            other = jnp.where(first_core, ok_down, ok_up)
            some = some | ok_up | ok_down
            flags += [own | upper, own & upper, other | upper, other & upper]
        return [some, upper, *flags]

    ok = z >= 4
    last = [ok, upper, jnp.where(first_core, ok | upper, ok & upper), jnp.where(first_core, ok & upper, ok | upper)]
    info = i32(core, image_here[0], 1, upper, *ahead, *valid_of(1), *valid_of(2), *valid_of(3), *last)
    gates = jnp.tanh(gate)

    text = jnp.concatenate([wide(text_q), wide(text_k), wide(text_v)], axis=2)
    text, vision_kv = lax.optimization_barrier((text, vision_kv))
    image, here = vision_kv[0], image_here[0] > 0
    n_vis = image.shape[1]
    flag = lambda f: jnp.full((FLAG_ROWS, HD), f, jnp.bfloat16)
    mine = jnp.where(first_core, image[0], image[1])
    pair = jnp.where(first_core, image[1], image[0])
    got = send(jnp.concatenate([pair, flag(here)]), swap)

    there = got[n_vis, 0] > 0
    latest = jnp.where(jnp.where(first_core, there, ~here), got[:n_vis], mine)
    latest = jnp.concatenate([latest, flag(here | there)])

    after = lax.optimization_barrier
    one_back = send(latest, later)
    q = spread(text)

    kv = q[:, G * HD :]
    groups = [[(x * 8 + p) * 2 + c for x in range(2) for c in range(2)] for p in range(8)]
    near = lax.all_gather(kv, "seq", axis=0, tiled=True, axis_index_groups=groups)
    ring = up + down
    near, one_back, info, gates = after((near, one_back, info, gates))
    two_back = send(one_back, later)
    load1 = send(near, ring)

    views = tuple(tuple((0, n * i, n, 2 + i) for i in range(m)) for m in (4, 2))
    state = self_step(info, 2, q, [near], views, None, None)
    def views_of(m):
        lower = [(i, 0, 2 * n, 2 + 2 * i) for i in range(m)]
        higher = [(i, 2 * n, 2 * n, 3 + 2 * i) for i in range(m)]
        return tuple(lower + higher), tuple(lower)

    load1, token = after((load1, state[2]))
    sib1 = send(load1, swap)
    load2 = send(load1, ring)
    state = self_step(info, 8, q, [load1, sib1], views_of(2), state, token)
    load2, token = after((load2, state[2]))
    sib2 = send(load2, swap)
    load3 = send(load2, ring)
    state = self_step(info, 14, q, [load2, sib2], views_of(2), state, token)
    load3, token = after((load3, state[2]))
    sib3 = send(load3, swap)
    far = send(core_half(info, load3), ring)
    state = self_step(info, 20, q, [load3, sib3], views_of(2), state, token)
    far, two_back, token = after((far, two_back, state[2]))
    far_sib = send(far, swap)
    keep, back = active_image(info, mine, got, one_back, two_back)
    back = send(back, swap)
    views = ((0, 0, 2 * n, 2), (1, 0, 2 * n, 3))
    state = self_step(info, 26, q, [far, far_sib], (views, views), state, token)
    out = cross_step(info, gates, q, keep, back, state)

    out = out.reshape(n_head, rows, -1)
    out = lax.all_to_all(out, "head", split_axis=0, concat_axis=0, tiled=True)
    return out.transpose(1, 0, 2).reshape(rows, -1)


def solution(mesh):
    placed = (
        P(("seq", "head"), None),
        P(("seq", "head"), None),
        P(("seq", "head"), None),
        P("seq", None, None, "head"),
        P("seq"),
        P("head"),
    )
    return jax.shard_map(
        local, mesh=mesh, in_specs=placed, out_specs=P(("seq", "head"), None), check_vma=False
    )
```

```python
import functools
import math

import jax
import jax.numpy as jnp
from jax import lax
from jax.experimental import pallas as pl
from jax.experimental.pallas import tpu as pltpu
from jax.sharding import PartitionSpec as P

HD = 128
G = 8
EXP2_SCALE = math.log2(math.e) / math.sqrt(HD)
NEG = -1e30
FLAG_ROWS = 16
TOKEN = jax.ShapeDtypeStruct((8, 128), jnp.float32)


def scores_of(q, keys):
    return lax.dot_general(q, keys, (((1,), (1,)), ((), ())), preferred_element_type=jnp.float32)


def sweep(rows, q_ref, parts, bufs, read, write):
    kbuf, vbuf = bufs[:2]
    scores, weights, tops = bufs[2:4], bufs[4:6], bufs[6:8]
    half = rows // 2
    spans = []
    at = 0
    for kv, _, _ in parts:
        n = kv.shape[0]
        kbuf[at : at + n] = kv[:, :HD]
        vbuf[at : at + n, :HD] = kv[:, HD:]
        spans.append(slice(at, at + n))
        at += n
    vbuf[:at, HD:] = jnp.ones((at, HD), jnp.bfloat16)

    def place(h, i):
        start = h * rows + i * half
        return pl.ds(start if isinstance(h, int) else pl.multiple_of(start, half), half)

    def score(h, i):
        lanes = h * HD if isinstance(h, int) else pl.multiple_of(h * HD, HD)
        q = q_ref[i * half : (i + 1) * half, pl.ds(lanes, HD)]
        s = scores_of(q, kbuf[:at])
        if parts[0][2] is None:
            scores[i][:, :at] = s
        else:
            for (_, _, ahead), span in zip(parts, spans):
                n = span.stop - span.start
                row = lax.broadcasted_iota(jnp.int32, (half, n), 0) + i * half
                col = lax.broadcasted_iota(jnp.int32, (half, n), 1)
                scores[i][:, span] = jnp.where(row - col >= ahead, s[:, span], NEG)

    def soften(h, i):
        old = read(place(h, i))
        top = None if old is None else old[0]
        for (_, valid, _), span in zip(parts, spans):
            t = jnp.broadcast_to(jnp.max(scores[i][:, span], axis=1, keepdims=True), (half, HD))
            if valid is not None:
                t = jnp.where(valid, t, NEG)
            top = t if top is None else jnp.maximum(top, t)
        tops[i][...] = jnp.broadcast_to(top, (half, HD))
        for (_, valid, _), span in zip(parts, spans):
            base = top[:, :1] * EXP2_SCALE
            if valid is not None:
                base = jnp.where(valid, base, -NEG)
            weights[i][:, span] = jnp.exp2(scores[i][:, span] * EXP2_SCALE - base).astype(jnp.bfloat16)

    def gather(h, i):
        pv = jnp.dot(weights[i][:, :at], vbuf[:at], preferred_element_type=jnp.float32)
        total, acc, top = pv[:, HD:], pv[:, :HD], tops[i][...]
        old = read(place(h, i))
        if old is not None:
            factor = jnp.exp2((old[0] - top) * EXP2_SCALE)
            total, acc = old[1] * factor + total, old[2] * factor + acc
        write(h, i, place(h, i), top, total, acc)

    score(0, 0)
    soften(0, 0)
    score(0, 1)

    def head(h, carry):
        gather(h, 0)
        soften(h, 1)
        score(h + 1, 0)
        gather(h, 1)
        soften(h + 1, 0)
        score(h + 1, 1)
        return carry

    for h in range(G - 1):
        head(h, 0)
    gather(G - 1, 0)
    soften(G - 1, 1)
    gather(G - 1, 1)


def scratch(rows, n_keys):
    half = rows // 2
    return [
        pltpu.VMEM((n_keys, HD), jnp.bfloat16),
        pltpu.VMEM((n_keys, 2 * HD), jnp.bfloat16),
        *[pltpu.VMEM((half, n_keys), jnp.float32)] * 2,
        *[pltpu.VMEM((half, n_keys), jnp.bfloat16)] * 2,
        *[pltpu.VMEM((half, HD), jnp.float32)] * 2,
    ]


def self_kernel(shape, valid_ref, q_ref, *refs):
    n_in, views, first, base = shape
    refs, bufs = refs[:-8], refs[-8:]
    kv_refs, refs = refs[:n_in], refs[n_in:]
    rows = q_ref.shape[0]
    half = rows // 2
    if not first:
        acc_in, ml_in, refs = refs[0], refs[1], refs[3:]
    acc_out, ml_out, token_ref = refs
    token_ref[...] = jnp.zeros_like(token_ref)

    def read(at):
        if first:
            return None
        return ml_in[0, at], ml_in[1, at], acc_in[at]

    def write(h, i, at, top, total, acc):
        acc_out[at] = acc
        ml_out[0, at] = top
        ml_out[1, at] = total

    def parts(group):
        return [
            (
                kv_refs[i].at[start : start + n],
                None if flag is None or first else valid_ref[base + flag] > 0,
                valid_ref[base + flag] if first else None,
            )
            for i, start, n, flag in views[group]
        ]

    any_a = valid_ref[base] > 0
    any_b = valid_ref[base + 1] > 0

    @pl.when(any_b)
    def _():
        sweep(rows, q_ref, parts(0), bufs, read, write)

    @pl.when(jnp.logical_and(jnp.logical_not(any_b), any_a))
    def _():
        sweep(rows, q_ref, parts(1), bufs, read, write)

    if not first:

        @pl.when(jnp.logical_not(jnp.logical_or(any_a, any_b)))
        def _():
            def head(h, carry):
                for i in range(2):
                    at = pl.ds(pl.multiple_of(h * rows + i * half, half), half)
                    top, total, acc = read(at)
                    write(h, i, at, top, total, acc)
                return carry

            lax.fori_loop(0, G, head, 0)


def self_step(valid, base, q, kvs, views, state, token):
    rows = q.shape[0]
    n_keys = sum(v[2] for v in views[0])
    first = state is None
    operands = [valid, q, *kvs]
    if not first:
        operands += list(state[:2])
    if not first:
        operands.append(token)
    outs = [jax.ShapeDtypeStruct((G * rows, HD), jnp.float32), jax.ShapeDtypeStruct((2, G * rows, HD), jnp.float32), TOKEN]
    whole = pl.BlockSpec(memory_space=pltpu.VMEM)
    return pl.pallas_call(
        functools.partial(self_kernel, (len(kvs), views, first, base)),
        out_shape=outs,
        in_specs=[pl.BlockSpec(memory_space=pltpu.SMEM)] + [whole] * (len(operands) - 1),
        out_specs=[whole] * 3,
        scratch_shapes=scratch(rows, n_keys),
        compiler_params=pltpu.CompilerParams(vmem_limit_bytes=VMEM),
        cost_estimate=pl.CostEstimate(
            flops=4 * G * rows * n_keys * HD * 2,
            bytes_accessed=G * 2 * rows * HD * 8 + n_keys * HD * 4,
            transcendentals=G * rows * n_keys,
        ),
    )(*operands)


VMEM = 20 << 20


def flag_of(ref):
    return jnp.max(ref[-FLAG_ROWS:, :].astype(jnp.float32)) > 0


def choose(index, sources, out_ref):
    n = sources[0].shape[0]
    for i, source in enumerate(sources):

        @pl.when(index == i)
        def _():
            out_ref[:n] = source[:n]


def active_kernel(info_ref, mine_ref, got_ref, one_ref, two_ref, keep_ref, back_ref):
    first_core, here = info_ref[0] == 0, info_ref[1] > 0
    there, one, two = flag_of(got_ref), flag_of(one_ref), flag_of(two_ref)
    n = mine_ref.shape[0]
    here0 = jnp.where(first_core, here, there)
    here1 = jnp.where(first_core, there, here)
    sources = (mine_ref, got_ref, one_ref, two_ref)
    carried = jnp.where(one, 2, 3)
    active0 = jnp.where(here0, jnp.where(first_core, 0, 1), carried)
    active1 = jnp.where(here1, jnp.where(first_core, 1, 0), active0)
    choose(jnp.where(first_core, active0, active1), sources, keep_ref)
    choose(jnp.where(first_core, active1, active0), sources, back_ref)
    earlier = jnp.logical_or(jnp.logical_or(one, two), here0)
    seen = jnp.logical_or(earlier, jnp.logical_and(jnp.logical_not(first_core), here1))
    keep_ref[n:] = jnp.full((FLAG_ROWS, HD), seen.astype(jnp.float32), jnp.float32).astype(jnp.bfloat16)


def active_image(info, mine, got, one, two):
    whole = pl.BlockSpec(memory_space=pltpu.VMEM)
    return pl.pallas_call(
        active_kernel,
        out_shape=[jax.ShapeDtypeStruct(x.shape, x.dtype) for x in (got, mine)],
        in_specs=[pl.BlockSpec(memory_space=pltpu.SMEM)] + [whole] * 4,
        out_specs=[whole] * 2,
        compiler_params=pltpu.CompilerParams(vmem_limit_bytes=2 << 20),
        cost_estimate=pl.CostEstimate(flops=0, bytes_accessed=2 << 20, transcendentals=0),
    )(info, mine, got, one, two)


def cross_kernel(info_ref, gate_ref, q_ref, keep_ref, back_ref, acc_ref, ml_ref, out_ref, kv, *bufs):
    rows = q_ref.shape[0]
    half = rows // 2
    n = back_ref.shape[0]
    first_core = info_ref[0] == 0
    seen = jnp.where(flag_of(keep_ref), 1.0, 0.0)

    @pl.when(first_core)
    def _():
        kv[:, :HD] = keep_ref[:n]
        kv[:, HD:] = back_ref[...]

    @pl.when(jnp.logical_not(first_core))
    def _():
        kv[:, :HD] = back_ref[...]
        kv[:, HD:] = keep_ref[:n]

    def write(h, i, at, top, total, acc):
        o = acc_ref[at] / ml_ref[1, at] + acc / total * (gate_ref[h] * seen)
        lanes = h * HD if isinstance(h, int) else pl.multiple_of(h * HD, HD)
        out_ref[i * half : (i + 1) * half, pl.ds(lanes, HD)] = o.astype(out_ref.dtype)

    sweep(rows, q_ref, [(kv, None, None)], bufs, lambda at: None, write)


def cross_step(info, gates, q, keep, back, state):
    rows, n = q.shape[0], back.shape[0]
    whole = pl.BlockSpec(memory_space=pltpu.VMEM)
    return pl.pallas_call(
        cross_kernel,
        out_shape=jax.ShapeDtypeStruct((rows, G * HD), jnp.bfloat16),
        in_specs=[pl.BlockSpec(memory_space=pltpu.SMEM)] * 2 + [whole] * 5,
        out_specs=whole,
        scratch_shapes=[pltpu.VMEM((n, 2 * HD), jnp.bfloat16)] + scratch(rows, n),
        compiler_params=pltpu.CompilerParams(vmem_limit_bytes=VMEM),
        cost_estimate=pl.CostEstimate(
            flops=4 * G * rows * n * HD * 2,
            bytes_accessed=G * rows * HD * 8 + n * HD * 4,
            transcendentals=G * rows * n,
        ),
    )(info, gates, q, keep, back, *state[:2])


def half_kernel(info_ref, load_ref, out_ref):
    n = out_ref.shape[0]
    for core in range(2):

        @pl.when(info_ref[0] == core)
        def _():
            out_ref[...] = load_ref[core * n : (core + 1) * n]


def core_half(info, load):
    whole = pl.BlockSpec(memory_space=pltpu.VMEM)
    return pl.pallas_call(
        half_kernel,
        out_shape=jax.ShapeDtypeStruct((load.shape[0] // 2, load.shape[1]), load.dtype),
        in_specs=[pl.BlockSpec(memory_space=pltpu.SMEM), whole],
        out_specs=whole,
        compiler_params=pltpu.CompilerParams(vmem_limit_bytes=2 << 20),
        cost_estimate=pl.CostEstimate(flops=0, bytes_accessed=1 << 20, transcendentals=0),
    )(info, load)


def lay_kernel(q_ref, k_ref, v_ref, out_ref):
    for h in range(out_ref.shape[0]):
        out_ref[h, :, : G * HD] = q_ref[:, h * G * HD : (h + 1) * G * HD]
        out_ref[h, :, G * HD : (G + 1) * HD] = k_ref[:, h * HD : (h + 1) * HD]
        out_ref[h, :, (G + 1) * HD :] = v_ref[:, h * HD : (h + 1) * HD]


def lay_out(q, k, v):
    whole = pl.BlockSpec(memory_space=pltpu.VMEM)
    return pl.pallas_call(
        lay_kernel,
        out_shape=jax.ShapeDtypeStruct((k.shape[1] // HD, q.shape[0], (G + 2) * HD), q.dtype),
        in_specs=[whole] * 3,
        out_specs=whole,
        compiler_params=pltpu.CompilerParams(vmem_limit_bytes=4 << 20),
        cost_estimate=pl.CostEstimate(flops=0, bytes_accessed=2 << 20, transcendentals=0),
    )(q, k, v)


def paths(n_seq, n_ring):
    def at(half, z, core):
        return (half * n_ring + z % n_ring) * 2 + core

    halves, zs = range(n_seq // (2 * n_ring)), range(n_ring)
    swap = [(i, i ^ 1) for i in range(n_seq)]
    up = [(at(x, z, 0), at(x, z + 1, 0)) for x in halves for z in zs]
    down = [(at(x, z, 1), at(x, z - 1, 1)) for x in halves for z in zs]
    return swap, up, down


def local(text_q, text_k, text_v, vision_kv, image_here, gate):
    send = lambda v, pairs: lax.ppermute(v, "seq", pairs)
    seq = lax.axis_index("seq")
    core, z, half = seq % 2, (seq // 2) % 8, seq // 16
    swap, up, down = paths(32, 8)
    later = [(i, i + 2) for i in range(30)]
    later_still = [(i, i + 4) for i in range(28)]
    first_core = core == 0
    i32 = lambda *v: jnp.stack([jnp.asarray(x, jnp.int32) for x in v])

    rows = text_q.shape[0]
    n_head = lax.axis_size("head")
    spread = lambda t: lax.all_to_all(t, "head", split_axis=0, concat_axis=0, tiled=True).reshape(n_head * rows, -1)
    n = n_head * rows
    upper = half == 1
    ahead = [((x * 8 + z) * 2 + c - seq) * n for x in range(2) for c in range(2)]
    def valid_of(*steps):
        some, flags = False, []
        for t in steps:
            ok_up, ok_down = z >= t, z + t >= 8
            own = jnp.where(first_core, ok_up, ok_down)
            other = jnp.where(first_core, ok_down, ok_up)
            some = some | ok_up | ok_down
            flags += [own | upper, own & upper, other | upper, other & upper]
        return [some, upper, *flags]

    ok = z >= 4
    last = [ok, upper, jnp.where(first_core, ok | upper, ok & upper), jnp.where(first_core, ok & upper, ok | upper)]
    info = i32(core, image_here[0], 1, upper, *ahead, *valid_of(1), *valid_of(2), *valid_of(3), *last)
    gates = jnp.tanh(gate)

    text = lay_out(text_q, text_k, text_v)
    text, vision_kv = lax.optimization_barrier((text, vision_kv))
    image, here = vision_kv[0], image_here[0] > 0
    n_vis = image.shape[1]
    flag = lambda f: jnp.full((FLAG_ROWS, HD), f, jnp.bfloat16)
    mine = jnp.where(first_core, image[0], image[1])
    pair = jnp.where(first_core, image[1], image[0])
    got = send(jnp.concatenate([pair, flag(here)]), swap)

    there = got[n_vis, 0] > 0
    latest = jnp.where(jnp.where(first_core, there, ~here), got[:n_vis], mine)
    latest = jnp.concatenate([latest, flag(here | there)])

    after = lax.optimization_barrier
    one_back = send(latest, later)
    q = spread(text)

    kv = q[:, G * HD :]
    groups = [[(x * 8 + p) * 2 + c for x in range(2) for c in range(2)] for p in range(8)]
    near = lax.all_gather(kv, "seq", axis=0, tiled=True, axis_index_groups=groups)
    ring = up + down
    near, one_back, info, gates = after((near, one_back, info, gates))
    two_back = send(one_back, later)
    load1 = send(near, ring)

    views = tuple(tuple((0, n * i, n, 2 + i) for i in range(m)) for m in (4, 2))
    state = self_step(info, 2, q, [near], views, None, None)
    def views_of(m):
        lower = [(i, 0, 2 * n, 2 + 2 * i) for i in range(m)]
        higher = [(i, 2 * n, 2 * n, 3 + 2 * i) for i in range(m)]
        return tuple(lower + higher), tuple(lower)

    load1, token = after((load1, state[2]))
    sib1 = send(load1, swap)
    load2 = send(load1, ring)
    state = self_step(info, 8, q, [load1, sib1], views_of(2), state, token)
    load2, token = after((load2, state[2]))
    sib2 = send(load2, swap)
    load3 = send(load2, ring)
    state = self_step(info, 14, q, [load2, sib2], views_of(2), state, token)
    load3, token = after((load3, state[2]))
    sib3 = send(load3, swap)
    far = send(core_half(info, load3), ring)
    state = self_step(info, 20, q, [load3, sib3], views_of(2), state, token)
    far, two_back, token = after((far, two_back, state[2]))
    far_sib = send(far, swap)
    keep, back = active_image(info, mine, got, one_back, two_back)
    back = send(back, swap)
    views = ((0, 0, 2 * n, 2), (1, 0, 2 * n, 3))
    state = self_step(info, 26, q, [far, far_sib], (views, views), state, token)
    out = cross_step(info, gates, q, keep, back, state)

    out = out.reshape(n_head, rows, -1)
    out = lax.all_to_all(out, "head", split_axis=0, concat_axis=0, tiled=True)
    return out.transpose(1, 0, 2).reshape(rows, -1)


def solution(mesh):
    placed = (
        P(("seq", "head"), None),
        P(("seq", "head"), None),
        P(("seq", "head"), None),
        P("seq", None, None, "head"),
        P("seq"),
        P("head"),
    )
    return jax.shard_map(
        local, mesh=mesh, in_specs=placed, out_specs=P(("seq", "head"), None), check_vma=False
    )
```
